32 devices in a mesh: grp: 2 (over y), smp: 8 (over z, x), par: 2 (over core).
Axes of the slice: x: 2, y: 2, z: 4, core: 2. Of those that a mesh axis runs over, the one named last changes fastest.
Arguments:
- log_derivs: bfloat16 [1536, 2048], P(('grp', 'smp'), 'par'), parts along dimension 0, may hold values from -1 to 1, as said below
- coeffs: float32 [1536], P(('grp', 'smp')), parts along dimension 0, may hold values from -6 to 6
Outputs:
- gram_band: float32 [1536, 480], P(('grp', 'smp'), 'par'), parts along dimension 0
- update: float32 [4096], P(('grp', 'par')), parts along dimension 0
The draws below stay inside these ranges and needn't reach their ends.
There are 2 independent parts, one for each index of `grp`. The reference program is written for one: setup_inputs(seed, part) draws one part's arguments, and reference() takes and returns one part's arrays. A program takes and returns all parts, laid end to end along the dimension named above; each array names one. Nothing has to cross between parts.
Inputs may be any that keep to these rules, and one draw needn't show every extreme that they name: `log_derivs`: entries of order a tenth.
All inputs are finite; a program needn't handle non-finite values.
Results may differ from the reference program's by a relative error of at most 0.0029.
Values may be sent and summed in bfloat16 or wider, within the bound.
A program may use at most 64 MiB of HBM per device.

```python
import jax
import jax.numpy as jnp
from jax import lax

S_DEV = 96
NS = 768
P_SIZE = 2048
HALF = 4
BAND = 480
N_SMP = 8


def draw_log_derivs(key, part):
    key = jax.random.fold_in(key, 11)
    key_off, key_noise, key_rows = jax.random.split(key, 3)
    offset = 0.05 * jax.random.normal(key_off, (1, P_SIZE), jnp.float32)
    noise = jax.random.normal(key_noise, (NS, P_SIZE), jnp.float32)
    rows = jnp.exp(jax.random.uniform(key_rows, (NS, 1), jnp.float32, -0.35, 0.35))
    values = jnp.clip(offset + 0.0221 * rows * noise, -1.0, 1.0)
    return values.astype(jnp.bfloat16)


def shard_levels(key, extent, cuts, least, largest):
    factor_of, own = 1.0, jax.random.fold_in(key, 6)
    for axis_at, blocks in cuts:
        draws = jnp.exp(jax.random.uniform(jax.random.fold_in(own, axis_at), (blocks,), jnp.float32, least / len(cuts), largest / len(cuts)))
        factor_of = factor_of * jnp.repeat(draws, extent[axis_at] // blocks).reshape([-1 if axis == axis_at else 1 for axis in range(len(extent))])
    return factor_of


def normal_values(rng, extent, scale, reach, cuts=(), kind=jnp.bfloat16):
    gain = shard_levels(rng, extent, cuts, -0.22, 0.18) if cuts else 1.0
    values = jax.random.normal(rng, extent, jnp.float32) * scale * gain
    return jnp.minimum(jnp.maximum(values, -reach), reach).astype(kind)


def setup_inputs(seed: int = 0, part: int = 0) -> dict:
    key_of = jax.random.split(jax.random.key(seed), 3)
    part_splits = jax.random.split(jax.random.fold_in(key_of[2], part), 3)
    log_derivs = draw_log_derivs(jax.random.fold_in(jax.random.fold_in(key_of[2], part), 71), part)
    coeffs = normal_values(part_splits[1], (NS,), 1.0, 6.0, ((0, 8),), jnp.float32)
    return dict(log_derivs=log_derivs, coeffs=coeffs)


def reference(log_derivs, coeffs):
    mean = jnp.sum(log_derivs.astype(jnp.float32), axis=0) / NS
    centred = (log_derivs.astype(jnp.float32) - mean).astype(jnp.bfloat16)
    update = jnp.dot(coeffs, centred.astype(jnp.float32), precision=lax.Precision.HIGHEST)
    blocks = centred.reshape(N_SMP, S_DEV, P_SIZE)
    offsets = jnp.arange(HALF + 1).astype(jnp.int32)

    def one_block(index):
        chosen = ((index + offsets) % N_SMP).astype(jnp.int32)
        others = blocks[chosen].astype(jnp.float32)
        own = blocks[index].astype(jnp.float32)
        tiles = jnp.einsum("sp,kqp->skq", own, others, precision=lax.Precision.HIGHEST)
        return tiles.reshape(S_DEV, (HALF + 1) * S_DEV)

    gram_band = lax.map(one_block, jnp.arange(N_SMP).astype(jnp.int32))
    return gram_band.reshape(NS, BAND), update
```

```python
import functools

import jax
import jax.numpy as jnp
from jax import lax
from jax.experimental import pallas as pl
from jax.experimental.pallas import tpu as pltpu
from jax.sharding import PartitionSpec as P

CHUNKS = 3
UNROLL = 16


def each(low, high, body):
    if high - low <= UNROLL:
        for step in range(low, high):
            body(step)
    else:
        lax.fori_loop(low, high, lambda step, _: (body(step), 0)[1], 0)


def kernel(
    count, x_hbm, c_ref, gram_ref, update_ref,
    slots, cent, stats, part, got,
    load_sem, stat_send, stat_recv, block_send, block_recv, swap_send, swap_recv,
):
    half = count // 2
    depth = half // 2
    rows, cols = slots.shape[1], slots.shape[2]
    width = part.shape[1]
    piece = rows // CHUNKS
    me = lax.axis_index("smp")
    core = lax.axis_index("par")
    bit = lax.rem(me, 2)

    def at(steps):
        return lax.rem(me + steps + count, count)

    load = pltpu.make_async_copy(x_hbm, slots.at[0], load_sem)
    load.start()
    barrier = pltpu.get_barrier_semaphore()
    each(1, count, lambda j: pl.semaphore_signal(barrier, inc=1, device_id={"smp": at(j)}))
    pl.semaphore_signal(barrier, inc=1, device_id={"par": 1 - core})

    c = c_ref[...]
    c1 = c.astype(jnp.bfloat16).astype(jnp.float32)
    c2 = (c - c1).astype(jnp.bfloat16).astype(jnp.float32)
    c3 = c - c1 - c2
    row = lax.broadcasted_iota(jnp.int32, (16, rows), 0)
    weights = jnp.where(row == 0, 1.0, jnp.where(row == 1, c1, jnp.where(row == 2, c2, jnp.where(row == 3, c3, 0.0))))
    load.wait()
    sums = jnp.dot(weights.astype(jnp.bfloat16), slots[0], preferred_element_type=jnp.float32)
    stats[me, 0:1, :] = sums[0:1]
    stats[me, 1:2, :] = sums[1:2] + sums[2:3] + sums[3:4]
    stats[me, 2:3, :] = jnp.broadcast_to(jnp.sum(c, axis=1, keepdims=True), (1, cols))
    stats[me, 3:4, :] = jnp.zeros((1, cols), jnp.float32)
    pl.semaphore_wait(barrier, count)

    def stat_copy(steps):
        return pltpu.make_async_remote_copy(
            src_ref=stats.at[me], dst_ref=stats.at[me],
            send_sem=stat_send.at[steps], recv_sem=stat_recv.at[me],
            device_id={"smp": at(steps)},
        )

    def stat_arrival(steps):
        other = at(steps)
        return pltpu.make_async_remote_copy(
            src_ref=stats.at[other], dst_ref=stats.at[other],
            send_sem=stat_send.at[steps], recv_sem=stat_recv.at[other],
            device_id={"smp": other},
        )

    def block_copy(source, target, chunk, steps):
        span = pl.ds(chunk * piece, piece)
        return pltpu.make_async_remote_copy(
            src_ref=slots.at[source, span], dst_ref=slots.at[target, span],
            send_sem=block_send.at[target, chunk], recv_sem=block_recv.at[target, chunk],
            device_id={"smp": at(steps)},
        )

    mate = 1 - 2 * bit
    each(1, count, lambda j: stat_copy(j).start())

    def send_column(d):
        for chunk in range(CHUNKS):
            block_copy(0, 2 * d, chunk, -2 * d).start()

    @pl.when(bit == 1)
    def _():
        for chunk in range(CHUNKS):
            block_copy(0, 1, chunk, -1).start()

    each(1, depth + 1, send_column)

    each(1, count, lambda j: stat_arrival(j).wait_recv())
    total = jnp.sum(stats[...], axis=0)
    mean = total[0:1] / (rows * count)
    update_ref[...] = total[1:2] - mean * total[2:3]

    def centre(k):
        value = (slots[k].astype(jnp.float32) - mean).astype(jnp.bfloat16)
        cent[pl.ds(pl.multiple_of(k * rows, 16), rows), :] = value

    centre(0)

    def column_arrival(d):
        for chunk in range(CHUNKS):
            block_copy(0, 2 * d, chunk, -2 * d).wait_recv()

            @pl.when(bit == 0)
            def _():
                block_copy(2 * d, 2 * d - 1, chunk, 1).start()

            @pl.when(jnp.logical_and(bit == 1, d < depth))
            def _():
                block_copy(2 * d, 2 * d + 1, chunk, -1).start()

        centre(2 * d)

    each(1, depth + 1, column_arrival)

    def row_arrival(e):
        for chunk in range(CHUNKS):
            block_copy(0, 2 * e - 1, chunk, mate).wait_recv()
        centre(2 * e - 1)

    each(1, depth + 1, row_arrival)

    def tiles(which):
        other = cent[pl.ds(pl.multiple_of(which * width, 16), width), :]
        return lax.dot_general(
            cent[0:rows, :], other, (((1,), (1,)), ((), ())), preferred_element_type=jnp.float32
        )

    part[...] = tiles(1 - core)
    swap = pltpu.make_async_remote_copy(
        src_ref=part, dst_ref=got, send_sem=swap_send, recv_sem=swap_recv, device_id={"par": 1 - core},
    )
    swap.start()
    mine = tiles(core)

    each(1, count, lambda j: stat_copy(j).wait_send())

    def finish(k):
        for chunk in range(CHUNKS):
            block_copy(0, k, chunk, -2).wait_send()

    each(1, half + 1, finish)
    swap.wait()
    gram_ref[...] = mine + got[...]


def on_device(log_derivs, coeffs):
    rows, cols = log_derivs.shape
    count = lax.axis_size("smp")
    half = count // 2
    width = (half + 1) * rows // lax.axis_size("par")
    block = rows * cols * 2
    gram, update = pl.pallas_call(
        functools.partial(kernel, count),
        out_shape=(
            jax.ShapeDtypeStruct((rows, width), jnp.float32),
            jax.ShapeDtypeStruct((1, cols), jnp.float32),
        ),
        in_specs=[pl.BlockSpec(memory_space=pl.ANY), pl.BlockSpec(memory_space=pltpu.VMEM)],
        out_specs=(pl.BlockSpec(memory_space=pltpu.VMEM), pl.BlockSpec(memory_space=pltpu.VMEM)),
        scratch_shapes=[
            pltpu.VMEM((half + 1, rows, cols), jnp.bfloat16),
            pltpu.VMEM(((half + 1) * rows, cols), jnp.bfloat16),
            pltpu.VMEM((count, 4, cols), jnp.float32),
            pltpu.VMEM((rows, width), jnp.float32),
            pltpu.VMEM((rows, width), jnp.float32),
            pltpu.SemaphoreType.DMA,
            pltpu.SemaphoreType.DMA((count,)),
            pltpu.SemaphoreType.DMA((count,)),
            pltpu.SemaphoreType.DMA((half + 1, CHUNKS)),
            pltpu.SemaphoreType.DMA((half + 1, CHUNKS)),
            pltpu.SemaphoreType.DMA,
            pltpu.SemaphoreType.DMA,
        ],
        compiler_params=pltpu.CompilerParams(
            collective_id=0,
            has_side_effects=True,
            vmem_limit_bytes=min(56, 12 + (half + 1)) * 2**20 if half > 16 else 16 * 2**20,
        ),
        cost_estimate=pl.CostEstimate(
            flops=4 * rows * cols * width, bytes_accessed=2 * block, transcendentals=0
        ),
    )(log_derivs, coeffs.reshape(1, rows))
    return gram, update.reshape(cols)


def solution(mesh):
    return jax.shard_map(
        on_device,
        mesh=mesh,
        in_specs=(P(("grp", "smp"), "par"), P(("grp", "smp"))),
        out_specs=(P(("grp", "smp"), "par"), P(("grp", "par"))),
        check_vma=False,
    )
```

```python
import functools

import jax
import jax.numpy as jnp
from jax import lax
from jax.experimental import pallas as pl
from jax.experimental.pallas import tpu as pltpu
from jax.sharding import PartitionSpec as P

CHUNKS = 3
UNROLL = 16


def each(low, high, body):
    if high - low <= UNROLL:
        for step in range(low, high):
            body(step)
    else:
        lax.fori_loop(low, high, lambda step, _: (body(step), 0)[1], 0)


def kernel(
    count, x_hbm, c_hbm, gram_ref, update_ref,
    slots, cent, c_ref, stats, part, got,
    load_sem, c_sem, sum_send, sum_recv, up_send, up_recv,
    down_send, entry_send, cross_send, block_recv, tile_send, tile_recv,
):
    half = count // 2
    depth = half // 2
    lines = count // 2
    middle = half // 2
    rows, cols = slots.shape[1], slots.shape[2]
    lanes = cols // 8
    width = gram_ref.shape[1]
    piece = rows // CHUNKS
    me = lax.axis_index("smp")
    core = lax.axis_index("par")
    line, bit = lax.div(me, 2), lax.rem(me, 2)
    mate = 1 - 2 * bit

    def at(steps):
        return lax.rem(me + steps + count, count)

    load = pltpu.make_async_copy(x_hbm, slots.at[0], load_sem)
    load.start()
    c_load = pltpu.make_async_copy(c_hbm, c_ref, c_sem)
    c_load.start()
    barrier = pltpu.get_barrier_semaphore()
    each(1, count, lambda j: pl.semaphore_signal(barrier, inc=1, device_id={"smp": at(j)}))
    pl.semaphore_signal(barrier, inc=1, device_id={"par": 1 - core})

    def pack(value):
        return jnp.concatenate([value[:, lanes * j : lanes * (j + 1)] for j in range(8)], axis=0)

    def unpack(value):
        return jnp.concatenate([value[j : j + 1, :] for j in range(8)], axis=1)

    load.wait()
    stats[0, me] = pack(jnp.sum(slots[0].astype(jnp.float32), axis=0, keepdims=True))
    c_load.wait()
    pl.semaphore_wait(barrier, count)

    def stat_copy(kind, source, steps):
        send, recv = ((sum_send, sum_recv), (up_send, up_recv))[kind]
        return pltpu.make_async_remote_copy(
            src_ref=stats.at[kind, source], dst_ref=stats.at[kind, source],
            send_sem=send.at[steps], recv_sem=recv.at[source],
            device_id={"smp": at(steps)},
        )

    def block_copy(source, target, chunk, send, device):
        span = pl.ds(pl.multiple_of(chunk * piece, 16), piece)
        return pltpu.make_async_remote_copy(
            src_ref=slots.at[source, span], dst_ref=slots.at[target, span],
            send_sem=send, recv_sem=block_recv.at[target, chunk],
            device_id={"smp": device},
        )

    def down(d, chunk):
        return block_copy(2 * d, 2 * d + 2, chunk, down_send.at[d, chunk], at(-2))

    def up(d, chunk):
        return block_copy(2 * d, 2 * d - 2, chunk, down_send.at[d, chunk], at(2))

    def entry(chunk):
        return block_copy(0, half, chunk, entry_send.at[chunk], at(-2 * depth))

    def cross(d, chunk):
        return block_copy(2 * d, 2 * d - mate, chunk, cross_send.at[d, chunk], at(mate))

    each(1, count, lambda j: stat_copy(0, me, j).start())

    for chunk in range(CHUNKS):
        @pl.when(bit == 1)
        def _():
            cross(0, chunk).start()

        @pl.when(line > 0)
        def _():
            down(0, chunk).start()

        @pl.when(line < depth)
        def _():
            entry(chunk).start()

    each(1, count, lambda j: stat_copy(0, at(j), j).wait_recv())
    mean = unpack(jnp.sum(stats[0], axis=0)) / (rows * count)

    def tile_copy(k, low, size):
        span = pl.ds(pl.multiple_of(low, 16), size)
        return pltpu.make_async_remote_copy(
            src_ref=part.at[span], dst_ref=got.at[span],
            send_sem=tile_send.at[k], recv_sem=tile_recv.at[k],
            device_id={"par": 1 - core},
        )

    def tile_whole(k):
        return tile_copy(k, k * rows, rows)

    def tile_split(side):
        return tile_copy(middle, middle * rows + side * (rows // 2), rows // 2)

    def process(k):
        value = (slots[k].astype(jnp.float32) - mean).astype(jnp.bfloat16)
        if isinstance(k, int) and k == 0:
            cent[...] = value
        span = pl.ds(pl.multiple_of(k * rows, 16), rows)
        part[span, :] = lax.dot_general(
            value, cent[...], (((1,), (1,)), ((), ())), preferred_element_type=jnp.float32
        )

        @pl.when(jnp.logical_or(jnp.logical_and(k > middle, core == 0), jnp.logical_and(k < middle, core == 1)))
        def _():
            tile_whole(k).start()

        @pl.when(k == middle)
        def _():
            tile_split(1 - core).start()

    process(0)

    c = c_ref[...]
    c1 = c.astype(jnp.bfloat16).astype(jnp.float32)
    c2 = (c - c1).astype(jnp.bfloat16).astype(jnp.float32)
    c3 = c - c1 - c2
    row = lax.broadcasted_iota(jnp.int32, (16, rows), 0)
    weights = jnp.where(row == 0, c1, jnp.where(row == 1, c2, jnp.where(row == 2, c3, 0.0)))
    sums = jnp.dot(weights.astype(jnp.bfloat16), cent[...], preferred_element_type=jnp.float32)
    stats[1, me] = pack(sums[0:1] + sums[1:2] + sums[2:3])
    each(1, count, lambda j: stat_copy(1, me, j).start())

    wraps = line + depth >= lines

    def arrival(step):
        d = jnp.where(wraps, depth - lax.rem(step, depth), 1 + lax.div(step, CHUNKS))
        chunk = jnp.where(wraps, lax.div(step, depth), lax.rem(step, CHUNKS))
        block_copy(2 * d, 2 * d, chunk, down_send.at[d, chunk], at(2)).wait_recv()
        inside = line + d < lines

        @pl.when(jnp.logical_or(bit == 0, d < depth))
        def _():
            cross(d, chunk).start()

        @pl.when(jnp.logical_and(inside, jnp.logical_and(d < depth, line > 0)))
        def _():
            down(d, chunk).start()

        @pl.when(jnp.logical_and(jnp.logical_not(inside), jnp.logical_and(d > 1, line < lines - 1)))
        def _():
            up(d, chunk).start()

    each(0, depth * CHUNKS, lambda step: arrival(jnp.int32(step)))

    def pair(e):
        process(2 * e)
        for chunk in range(CHUNKS):
            block_copy(0, 2 * e - 1, chunk, entry_send.at[chunk], at(mate)).wait_recv()
        process(2 * e - 1)

    each(1, depth + 1, pair)

    for chunk in range(CHUNKS):
        @pl.when(line > 0)
        def _():
            down(0, chunk).wait_send()

        @pl.when(line < depth)
        def _():
            entry(chunk).wait_send()

        @pl.when(bit == 1)
        def _():
            cross(0, chunk).wait_send()

    def leave(d):
        inside = line + d < lines
        for chunk in range(CHUNKS):
            @pl.when(jnp.logical_or(bit == 0, d < depth))
            def _():
                cross(d, chunk).wait_send()

            @pl.when(jnp.logical_and(inside, jnp.logical_and(d < depth, line > 0)))
            def _():
                down(d, chunk).wait_send()

            @pl.when(jnp.logical_and(jnp.logical_not(inside), jnp.logical_and(d > 1, line < lines - 1)))
            def _():
                up(d, chunk).wait_send()

    each(1, depth + 1, leave)
    each(1, count, lambda j: stat_copy(0, me, j).wait_send())
    each(1, count, lambda j: stat_copy(1, me, j).wait_send())
    each(1, count, lambda j: stat_copy(1, at(j), j).wait_recv())
    update_ref[...] = unpack(jnp.sum(stats[1], axis=0))

    def swapped(k):
        @pl.when(jnp.logical_or(jnp.logical_and(k > middle, core == 0), jnp.logical_and(k < middle, core == 1)))
        def _():
            tile_whole(k).wait_send()

        @pl.when(jnp.logical_or(jnp.logical_and(k > middle, core == 1), jnp.logical_and(k < middle, core == 0)))
        def _():
            tile_whole(k).wait_recv()

        @pl.when(k == middle)
        def _():
            tile_split(1 - core).wait_send()
            tile_split(core).wait_recv()

    each(0, half + 1, swapped)
    mine = pl.ds(pl.multiple_of(core * width, 16), width)
    gram_ref[...] = (part[mine, :] + got[mine, :]).T


def on_device(log_derivs, coeffs):
    rows, cols = log_derivs.shape
    count = lax.axis_size("smp")
    half = count // 2
    depth = half // 2
    band = (half + 1) * rows
    width = band // lax.axis_size("par")
    block = rows * cols * 2
    dma = pltpu.SemaphoreType.DMA
    gram, update = pl.pallas_call(
        functools.partial(kernel, count),
        out_shape=(
            jax.ShapeDtypeStruct((rows, width), jnp.float32),
            jax.ShapeDtypeStruct((1, cols), jnp.float32),
        ),
        in_specs=[pl.BlockSpec(memory_space=pltpu.HBM)] * 2,
        out_specs=(pl.BlockSpec(memory_space=pltpu.VMEM), pl.BlockSpec(memory_space=pltpu.VMEM)),
        scratch_shapes=[
            pltpu.VMEM((half + 1, rows, cols), jnp.bfloat16),
            pltpu.VMEM((rows, cols), jnp.bfloat16),
            pltpu.VMEM((1, rows), jnp.float32),
            pltpu.VMEM((2, count, 8, cols // 8), jnp.float32),
            pltpu.VMEM((band, rows), jnp.float32),
            pltpu.VMEM((band, rows), jnp.float32),
            dma, dma,
            dma((count,)), dma((count,)), dma((count,)), dma((count,)),
            dma((depth + 1, CHUNKS)), dma((CHUNKS,)), dma((depth + 1, CHUNKS)),
            dma((half + 1, CHUNKS)), dma((half + 1,)), dma((half + 1,)),
        ],
        compiler_params=pltpu.CompilerParams(
            collective_id=0,
            has_side_effects=True,
            vmem_limit_bytes=48 * 2**20 if half > 16 else 16 * 2**20,
        ),
        cost_estimate=pl.CostEstimate(
            flops=4 * rows * cols * width, bytes_accessed=2 * block, transcendentals=0
        ),
    )(log_derivs, coeffs.reshape(1, rows))
    return gram, update.reshape(cols)


def solution(mesh):
    return jax.shard_map(
        on_device,
        mesh=mesh,
        in_specs=(P(("grp", "smp"), "par"), P(("grp", "smp"))),
        out_specs=(P(("grp", "smp"), "par"), P(("grp", "par"))),
        check_vma=False,
    )
```

```python
import functools

import jax
import jax.numpy as jnp
from jax import lax
from jax.experimental import pallas as pl
from jax.experimental.pallas import tpu as pltpu
from jax.sharding import PartitionSpec as P

CHUNKS = 6
FIRST = 2
MEAN_AFTER = 4
UNROLL = 16


def each(low, high, body):
    if high - low <= UNROLL:
        for step in range(low, high):
            body(step)
    else:
        lax.fori_loop(low, high, lambda step, _: (body(step), 0)[1], 0)


def kernel(
    count, x_hbm, c_hbm, gram_ref, update_ref,
    slots, cent, c_ref, pairs, stats, parts, band, spare,
    load_sem, c_sem, above, below, pair_send, pair_recv, stat_send, stat_recv, parts_send, parts_recv,
    down_send, entry_send, cross_send, block_recv, tile_send, tile_recv, spare_send, spare_recv,
):
    half = count // 2
    depth = half // 2
    lines = count // 2
    middle = half // 2
    rows, cols = slots.shape[1], slots.shape[2]
    lanes = cols // 8
    width = gram_ref.shape[1]
    piece = rows // CHUNKS
    me = lax.axis_index("smp")
    core = lax.axis_index("par")
    line, bit = lax.div(me, 2), lax.rem(me, 2)
    mate = 1 - 2 * bit

    def at(steps):
        return lax.rem(me + steps + count, count)

    load = pltpu.make_async_copy(x_hbm, slots.at[0], load_sem)
    load.start()
    c_load = pltpu.make_async_copy(c_hbm, c_ref, c_sem)
    c_load.start()
    barrier = pltpu.get_barrier_semaphore()
    pl.semaphore_signal(barrier, inc=1, device_id={"par": 1 - core})
    pl.semaphore_signal(barrier, inc=1, device_id={"smp": at(mate)})
    pl.semaphore_signal(barrier, inc=1, device_id={"smp": at(mate), "par": 1 - core})

    @pl.when(line > 0)
    def _():
        pl.semaphore_signal(barrier, inc=1, device_id={"smp": at(-2)})

    @pl.when(line < lines - 1)
    def _():
        pl.semaphore_signal(barrier, inc=1, device_id={"smp": at(2)})

    def pack(value):
        return jnp.concatenate([value[:, lanes * j : lanes * (j + 1)] for j in range(8)], axis=0)

    def unpack(value):
        return jnp.concatenate([value[j : j + 1, :] for j in range(8)], axis=1)

    load.wait()
    pairs[bit] = pack(jnp.sum(slots[0].astype(jnp.float32), axis=0, keepdims=True))
    c_load.wait()
    pl.semaphore_wait(barrier, 3 + jnp.where(line > 0, 1, 0) + jnp.where(line < lines - 1, 1, 0))

    def pair_copy(source):
        return pltpu.make_async_remote_copy(
            src_ref=pairs.at[source], dst_ref=pairs.at[source],
            send_sem=pair_send, recv_sem=pair_recv, device_id={"smp": at(mate)},
        )

    def line_copy(slot, steps):
        return pltpu.make_async_remote_copy(
            src_ref=stats.at[slot], dst_ref=stats.at[slot],
            send_sem=stat_send.at[steps], recv_sem=stat_recv.at[slot],
            device_id={"smp": at(2 * steps)},
        )

    def parts_copy(slot, steps):
        return pltpu.make_async_remote_copy(
            src_ref=parts.at[slot], dst_ref=parts.at[slot],
            send_sem=parts_send.at[steps], recv_sem=parts_recv.at[slot],
            device_id={"smp": at(steps)},
        )

    def block_copy(source, target, chunk, send, device):
        span = pl.ds(pl.multiple_of(chunk * piece, 16), piece)
        return pltpu.make_async_remote_copy(
            src_ref=slots.at[source, span], dst_ref=slots.at[target, span],
            send_sem=send, recv_sem=block_recv.at[target, chunk],
            device_id={"smp": device},
        )

    def down(d, chunk):
        return block_copy(d, d + 1, chunk, down_send.at[d, chunk], at(-2))

    def up(d, chunk):
        return block_copy(d, d - 1, chunk, down_send.at[d, chunk], at(2))

    def entry(chunk):
        return block_copy(0, depth, chunk, entry_send.at[chunk], at(-2 * depth))

    def cross(chunk):
        return block_copy(0, depth + 1, chunk, cross_send.at[chunk], at(mate))

    pair_copy(bit).start()

    @pl.when(line > 0)
    def _():
        for chunk in range(FIRST):
            down(0, chunk).start()

    def tell(q):
        @pl.when(line + q < lines)
        def _():
            if q > 1:
                pl.semaphore_wait(above.at[q - 1], 1)

            @pl.when(line > 0)
            def _():
                pl.semaphore_signal(above.at[q], inc=1, device_id={"smp": at(-2)})

        @pl.when(line - q >= 0)
        def _():
            if q > 1:
                pl.semaphore_wait(below.at[q - 1], 1)

            @pl.when(line < lines - 1)
            def _():
                pl.semaphore_signal(below.at[q], inc=1, device_id={"smp": at(2)})

    for q in range(1, depth + 1):
        tell(q)

    @pl.when(line < depth)
    def _():
        for chunk in range(FIRST):
            entry(chunk).start()

    for q in range(depth + 1, lines):
        tell(q)

    pair_copy(1 - bit).wait_recv()
    stats[line] = pairs[0] + pairs[1]
    each(1, lines, lambda j: line_copy(line, j).start())
    for chunk in range(FIRST, CHUNKS):
        @pl.when(line > 0)
        def _():
            down(0, chunk).start()

        @pl.when(line < depth)
        def _():
            entry(chunk).start()

    for chunk in range(CHUNKS):
        cross(chunk).start()

    def line_at(steps):
        return lax.rem(line + steps, lines)

    def mean_row():
        return unpack(jnp.sum(stats[...], axis=0)) / (rows * count)

    def tile_copy(k, source, low, size):
        span = pl.ds(pl.multiple_of(low, 16), size)
        return pltpu.make_async_remote_copy(
            src_ref=band.at[source, span], dst_ref=band.at[source, span],
            send_sem=tile_send.at[k], recv_sem=tile_recv.at[k],
            device_id={"par": 1 - core},
        )

    def tile_whole(k, source):
        return tile_copy(k, source, k * rows, rows)

    def tile_split(side, source):
        return tile_copy(middle, source, middle * rows + side * (rows // 2), rows // 2)

    def spare_copy(d, tile, source):
        return pltpu.make_async_remote_copy(
            src_ref=spare.at[d],
            dst_ref=band.at[source, pl.ds(pl.multiple_of(tile * rows, 16), rows)],
            send_sem=spare_send.at[d], recv_sem=spare_recv.at[tile, source],
            device_id={"smp": at(mate), "par": jnp.where(tile > middle, 1, 0)},
        )

    def for_mate(d):
        return jnp.logical_or(jnp.logical_and(bit == 0, d > 0), jnp.logical_and(bit == 1, d < depth))

    def centre(d, mean):
        return (slots[d].astype(jnp.float32) - mean).astype(jnp.bfloat16)

    def tile_of(value, which):
        return lax.dot_general(
            value, cent[which], (((1,), (1,)), ((), ())), preferred_element_type=jnp.float32
        )

    def process(d, mean):
        k = 2 * d
        value = centre(d, mean)

        @pl.when(for_mate(d))
        def _():
            spare[d] = tile_of(value, 1)
            spare_copy(d, k - mate, core).start()

        span = pl.ds(pl.multiple_of(k * rows, 16), rows)
        band[core, span] = tile_of(value, 0)

        @pl.when(jnp.logical_or(jnp.logical_and(k > middle, core == 0), jnp.logical_and(k < middle, core == 1)))
        def _():
            tile_whole(k, core).start()

        @pl.when(k == middle)
        def _():
            tile_split(1 - core, core).start()

    def middle_work():
        each(1, lines, lambda j: line_copy(line_at(j), j).wait_recv())
        mean = mean_row()
        cent[0] = centre(0, mean)
        c = c_ref[...]
        c1 = c.astype(jnp.bfloat16).astype(jnp.float32)
        c2 = (c - c1).astype(jnp.bfloat16).astype(jnp.float32)
        c3 = c - c1 - c2
        row = lax.broadcasted_iota(jnp.int32, (16, rows), 0)
        weights = jnp.where(row == 0, c1, jnp.where(row == 1, c2, jnp.where(row == 2, c3, 0.0)))
        sums = jnp.dot(weights.astype(jnp.bfloat16), cent[0], preferred_element_type=jnp.float32)
        parts[me] = pack(sums[0:1] + sums[1:2] + sums[2:3])
        each(1, count, lambda j: parts_copy(me, j).start())
        for chunk in range(CHUNKS):
            cross(chunk).wait_recv()
        cent[1] = centre(depth + 1, mean)
        process(0, mean)

    wraps = line + depth >= lines

    def arrival(step):
        d = jnp.where(wraps, depth - lax.rem(step, depth), 1 + lax.div(step, CHUNKS))
        chunk = jnp.where(wraps, lax.div(step, depth), lax.rem(step, CHUNKS))
        block_copy(d, d, chunk, down_send.at[d, chunk], at(2)).wait_recv()
        inside = line + d < lines

        @pl.when(jnp.logical_and(inside, jnp.logical_and(d < depth, line > 0)))
        def _():
            down(d, chunk).start()

        @pl.when(jnp.logical_and(jnp.logical_not(inside), jnp.logical_and(d > 1, line < lines - 1)))
        def _():
            up(d, chunk).start()

    each(0, MEAN_AFTER, lambda step: arrival(jnp.int32(step)))
    middle_work()
    each(MEAN_AFTER, depth * CHUNKS, lambda step: arrival(jnp.int32(step)))
    mean = mean_row()

    each(1, depth + 1, lambda d: process(d, mean))

    for chunk in range(CHUNKS):
        @pl.when(line > 0)
        def _():
            down(0, chunk).wait_send()

        @pl.when(line < depth)
        def _():
            entry(chunk).wait_send()

        cross(chunk).wait_send()

    def leave(d):
        inside = line + d < lines
        for chunk in range(CHUNKS):
            @pl.when(jnp.logical_and(inside, jnp.logical_and(d < depth, line > 0)))
            def _():
                down(d, chunk).wait_send()

            @pl.when(jnp.logical_and(jnp.logical_not(inside), jnp.logical_and(d > 1, line < lines - 1)))
            def _():
                up(d, chunk).wait_send()

    each(1, depth + 1, leave)
    pair_copy(bit).wait_send()
    each(1, lines, lambda j: line_copy(line, j).wait_send())
    each(1, count, lambda j: parts_copy(me, j).wait_send())
    each(1, count, lambda j: parts_copy(at(j), j).wait_recv())
    update_ref[...] = unpack(jnp.sum(parts[...], axis=0))

    def swapped(d):
        k = 2 * d

        @pl.when(for_mate(d))
        def _():
            spare_copy(d, k - mate, core).wait_send()

        @pl.when(jnp.logical_or(jnp.logical_and(k > middle, core == 0), jnp.logical_and(k < middle, core == 1)))
        def _():
            tile_whole(k, core).wait_send()

        @pl.when(jnp.logical_or(jnp.logical_and(k > middle, core == 1), jnp.logical_and(k < middle, core == 0)))
        def _():
            tile_whole(k, 1 - core).wait_recv()

        @pl.when(k == middle)
        def _():
            tile_split(1 - core, core).wait_send()
            tile_split(core, 1 - core).wait_recv()

        @pl.when(jnp.logical_and(d > 0, core == jnp.where(k - 1 > middle, 1, 0)))
        def _():
            for source in range(2):
                spare_copy(d, k - 1, source).wait_recv()

    each(0, depth + 1, swapped)
    mine = pl.ds(pl.multiple_of(core * width, 16), width)
    gram_ref[...] = (band[0, mine] + band[1, mine]).T


def on_device(log_derivs, coeffs):
    rows, cols = log_derivs.shape
    count = lax.axis_size("smp")
    half = count // 2
    depth = half // 2
    lines = count // 2
    band = (half + 1) * rows
    width = band // lax.axis_size("par")
    block = rows * cols * 2
    dma = pltpu.SemaphoreType.DMA
    gram, update = pl.pallas_call(
        functools.partial(kernel, count),
        out_shape=(
            jax.ShapeDtypeStruct((rows, width), jnp.float32),
            jax.ShapeDtypeStruct((1, cols), jnp.float32),
        ),
        in_specs=[pl.BlockSpec(memory_space=pltpu.HBM)] * 2,
        out_specs=(pl.BlockSpec(memory_space=pltpu.VMEM), pl.BlockSpec(memory_space=pltpu.VMEM)),
        scratch_shapes=[
            pltpu.VMEM((depth + 2, rows, cols), jnp.bfloat16),
            pltpu.VMEM((2, rows, cols), jnp.bfloat16),
            pltpu.VMEM((1, rows), jnp.float32),
            pltpu.VMEM((2, 8, cols // 8), jnp.float32),
            pltpu.VMEM((lines, 8, cols // 8), jnp.float32),
            pltpu.VMEM((count, 8, cols // 8), jnp.float32),
            pltpu.VMEM((2, band, rows), jnp.float32),
            pltpu.VMEM((depth + 1, rows, rows), jnp.float32),
            dma, dma,
            pltpu.SemaphoreType.REGULAR((lines,)), pltpu.SemaphoreType.REGULAR((lines,)),
            dma, dma, dma((lines,)), dma((lines,)), dma((count,)), dma((count,)),
            dma((depth + 1, CHUNKS)), dma((CHUNKS,)), dma((CHUNKS,)),
            dma((depth + 2, CHUNKS)), dma((half + 1,)), dma((half + 1,)),
            dma((depth + 1,)), dma((half + 1, 2)),
        ],
        compiler_params=pltpu.CompilerParams(
            collective_id=0,
            has_side_effects=True,
            vmem_limit_bytes=48 * 2**20 if half > 16 else 16 * 2**20,
        ),
        cost_estimate=pl.CostEstimate(
            flops=4 * rows * cols * width, bytes_accessed=2 * block, transcendentals=0
        ),
    )(log_derivs, coeffs.reshape(1, rows))
    return gram, update.reshape(cols)


def solution(mesh):
    return jax.shard_map(
        on_device,
        mesh=mesh,
        in_specs=(P(("grp", "smp"), "par"), P(("grp", "smp"))),
        out_specs=(P(("grp", "smp"), "par"), P(("grp", "par"))),
        check_vma=False,
    )
```
